128 devices in a mesh: row: 8 (over x, z_lo), col: 4 (over z_hi, core), depth: 4 (over y).
Axes of the slice: x: 4, y: 4, z: 4 (z_hi: 2, z_lo: 2; z = z_hi * 2 + z_lo), core: 2. Of those that a mesh axis runs over, the one named last changes fastest.
Arguments:
- out_grad: bfloat16 [131072, 512], P(('row', 'col'), 'depth'), may hold values from -6 to 6
- relu_mask: int32 [131072, 512], P(('row', 'col'), 'depth'), may hold values 0 or 1
- aggregated: bfloat16 [131072, 512], P(('row', 'col'), 'depth'), may hold values from -0.015625 to 0.015625
- weight: bfloat16 [512, 512], P(None, 'depth'), may hold values from -0.25 to 0.25
- tile_values: bfloat16 [8, 4, 544, 128, 128], P('row', 'col'), may hold values from -0.1875 to 0.1875
- tile_rows: int32 [8, 4, 544], P('row', 'col'), may hold values from 0 to 127, as said below
- tile_cols: int32 [8, 4, 544], P('row', 'col'), may hold values from 0 to 1023, as said below
- tile_count: int32 [8, 4], P('row', 'col'), may hold values from 0 to 544, as said below
Outputs:
- grad_input: bfloat16 [131072, 512], P(('row', 'col'), 'depth')
- grad_weight: float32 [512, 512], P(None, 'depth')
The draws below stay inside these ranges and needn't reach their ends.
Inputs may be any that keep to these rules, and one draw needn't show every extreme that they name: Slots below a device's count hold distinct tiles of the band: tile_cols is (r * 128 + tile_rows + k) mod 1024 for some k from -8 to 8, and tile_cols % 4 equals the device's col index c; slots at or after the count hold other coordinates of the same ranges and are to be ignored. `tile_cols`: see tile_rows. `tile_count`: some device is full in every draw.
All inputs are finite; a program needn't handle non-finite values. No bound on the sum of `relu_mask` on one device may be relied on, other than what follows from the above.
Results may differ from the reference program's by a relative error of at most 0.0049.
Values may be sent and summed in bfloat16 or wider, within the bound.
No kernel may reach another device: no remote copies, remote signals or barrier semaphores. Data moves between devices by JAX's collectives and lax.ppermute only.
A program may use at most 192 MiB of HBM per device.

```python
import jax
import jax.numpy as jnp
from jax import lax

F = 512
TILE = 128
BW = 8
RB = 128
CAP = 544
NBLK = 1024
NODES = 131072
N_ROW = 8
N_COL = 4


def tile_layout(key):
    band_span = 2 * BW + 1
    candidates = RB * band_span
    position = jnp.arange(candidates, dtype=jnp.int32)
    local_row = position // band_span
    band_shift = position % band_span - BW
    stripe_ids = jnp.arange(N_ROW, dtype=jnp.int32)[:, None, None]
    residues = jnp.arange(N_COL, dtype=jnp.int32)[None, :, None]
    col_block = (stripe_ids * RB + local_row[None, None, :] + band_shift[None, None, :]) % NBLK
    matches = col_block % N_COL == residues
    keep_key, full_key, chance_key = jax.random.split(key, 3)
    threshold = jax.random.randint(keep_key, (N_ROW, N_COL, 1), 100, 800)
    full_device = jax.random.randint(full_key, (), 0, N_ROW * N_COL)
    device_ids = jnp.arange(N_ROW * N_COL, dtype=jnp.int32).reshape(N_ROW, N_COL, 1)
    threshold = jnp.where(device_ids == full_device, 1000, threshold)
    chance = jax.random.randint(chance_key, (N_ROW, N_COL, candidates), 0, 1000)
    kept_tile = matches & (chance < threshold)
    sort_key = jnp.where(kept_tile, 0, 1) * candidates + position[None, None, :]
    slot_order = jnp.argsort(sort_key, axis=-1, stable=True)[..., :CAP]
    all_rows = jnp.broadcast_to(local_row[None, None, :], (N_ROW, N_COL, candidates))
    all_cols = jnp.broadcast_to(col_block, (N_ROW, N_COL, candidates))
    rows_out = jnp.take_along_axis(all_rows, slot_order, axis=-1)
    cols_out = jnp.take_along_axis(all_cols, slot_order, axis=-1)
    live_count = jnp.sum(kept_tile.astype(jnp.int32), axis=-1)
    return (rows_out.astype(jnp.int32), cols_out.astype(jnp.int32), live_count.astype(jnp.int32))


def draw_tile_rows(key, part):
    return tile_layout(key)[0]


def draw_tile_cols(key, part):
    return tile_layout(key)[1]


def draw_tile_count(key, part):
    return tile_layout(key)[2]


def with_ends(entries, key, least, top_value):
    spot = [jax.random.randint(jax.random.fold_in(key, axis), (), 0, length) for axis, length in enumerate(entries.shape)]
    widest = entries.shape.index(max(entries.shape))
    neighbour = spot[:widest] + [(spot[widest] + 1) % entries.shape[widest]] + spot[widest + 1:]
    return entries.at[tuple(spot)].set(least).at[tuple(neighbour)].set(top_value)


def block_scale(rng, extent, cuts, least, high):
    factor_of, own = 1.0, jax.random.fold_in(rng, 6)
    for dim, shards_of in cuts:
        steps = jnp.exp(jax.random.uniform(jax.random.fold_in(own, dim), (shards_of,), jnp.float32, least / len(cuts), high / len(cuts)))
        factor_of = factor_of * jnp.repeat(steps, extent[dim] // shards_of).reshape([-1 if axis == dim else 1 for axis in range(len(extent))])
    return factor_of


def normal_values(stream_key, dims, scale, bound, cuts=(), kind=jnp.bfloat16):
    drawn = scale * jax.random.normal(stream_key, dims, jnp.float32)
    if cuts:
        drawn = drawn * block_scale(stream_key, dims, cuts, -0.22, 0.18)
    return jnp.clip(drawn, -bound, bound).astype(kind)


def setup_inputs(seed: int = 0) -> dict:
    key_list = jax.random.split(jax.random.key(seed), 9)
    out_grad = normal_values(key_list[0], (NODES, F), 1.0, 6.0, ((0, 32), (1, 4)))
    relu_mask = with_ends((jax.random.randint(key_list[1], (NODES, F), 0, 2) < 1).astype(jnp.int32), jax.random.fold_in(key_list[1], 1), 0, 1)
    aggregated = normal_values(key_list[2], (NODES, F), NODES ** -0.5, 0.015625, ((0, 32), (1, 4)))
    weight = normal_values(key_list[3], (F, F), F ** -0.5, 0.25, ((1, 4),))
    tile_values = normal_values(key_list[4], (N_ROW, N_COL, CAP, TILE, TILE), (TILE * (2 * BW + 1) // 2) ** -0.5, 0.1875, ((0, 8), (1, 4)))
    tile_rows = draw_tile_rows(jax.random.fold_in(key_list[8], 71), 0)
    tile_cols = draw_tile_cols(jax.random.fold_in(key_list[8], 71), 0)
    tile_count = draw_tile_count(jax.random.fold_in(key_list[8], 71), 0)
    return dict(out_grad=out_grad, relu_mask=relu_mask, aggregated=aggregated, weight=weight, tile_values=tile_values, tile_rows=tile_rows, tile_cols=tile_cols, tile_count=tile_count)


def block_place(blocks, col_blocks):
    within = blocks % RB
    return ((blocks // RB) * RB + (within % N_COL) * col_blocks + within // N_COL).astype(jnp.int32)


def reference(out_grad, relu_mask, aggregated, weight, tile_values, tile_rows, tile_cols, tile_count):
    out_masked = out_grad * relu_mask.astype(jnp.bfloat16)
    col_blocks = RB // N_COL
    grad_blocks = out_masked.reshape(NBLK, TILE, F)
    slot_index = jnp.arange(CAP, dtype=jnp.int32)

    def device_pass(totals, device_data):
        values, row_index, col_index, live_count, stripe_id = device_data
        global_rows = stripe_id * RB + row_index
        picked = grad_blocks[block_place(global_rows, col_blocks)].astype(jnp.float32)
        picked = jnp.where((slot_index < live_count)[:, None, None], picked, jnp.zeros_like(picked))
        contrib = jnp.einsum('sij,sif->sjf', values.astype(jnp.float32), picked)
        totals = totals.at[block_place(col_index, col_blocks)].add(contrib)
        return totals, jnp.zeros((), jnp.float32)

    stripes = jnp.repeat(jnp.arange(N_ROW, dtype=jnp.int32), N_COL)
    scanned = lax.scan(device_pass, jnp.zeros((NBLK, TILE, F), jnp.float32),
                       (tile_values.reshape(N_ROW * N_COL, CAP, TILE, TILE),
                        tile_rows.reshape(N_ROW * N_COL, CAP).astype(jnp.int32),
                        tile_cols.reshape(N_ROW * N_COL, CAP).astype(jnp.int32),
                        tile_count.reshape(N_ROW * N_COL).astype(jnp.int32),
                        stripes))
    spread = scanned[0].reshape(NODES, F).astype(jnp.bfloat16)
    grad_input = jnp.dot(spread, weight.T, preferred_element_type=jnp.float32).astype(jnp.bfloat16)
    grad_weight = jnp.dot(aggregated.T, out_masked, preferred_element_type=jnp.float32)
    return grad_input, grad_weight
```

```python
import jax
import jax.numpy as jnp
from jax import lax
from jax.experimental import pallas as pl
from jax.experimental.pallas import tpu as pltpu
from jax.sharding import PartitionSpec as P

BW = 8
RB = 128
NBLK = 1024
T = 128
QUADS = 8
SLOTS = 5
RC = ("row", "col")
RD = ("row", "depth")
bf16 = jnp.bfloat16
f32 = jnp.float32


def ring(n, shift):
    return [(i, (i + shift) % n) for i in range(n)]


def flip(bit):
    return [(i, i ^ bit) for i in range(4)]


def params(mib):
    return pltpu.CompilerParams(vmem_limit_bytes=mib << 20)


SMEM = pl.BlockSpec(memory_space=pltpu.SMEM)
VMEM = pl.BlockSpec(memory_space=pltpu.VMEM)


def densify_kernel(inv, *refs):
    out = refs[-1]
    q = pl.program_id(0)
    for k in range(SLOTS * 4):
        slot, e = k // 4, k % 4
        tile = refs[k][0, 0, 0]
        live = inv[q * (SLOTS * 4) + k] >= 0
        turned = jnp.where(live, tile.T, jnp.zeros((T, T), bf16))
        out[0, slot * T:(slot + 1) * T, e * T:(e + 1) * T] = turned


def densify(inv, tile_values):
    def spec(k):
        return pl.BlockSpec(
            (1, 1, 1, T, T), lambda q, inv: (0, 0, jnp.maximum(inv[q * (SLOTS * 4) + k], 0), 0, 0)
        )

    return pl.pallas_call(
        densify_kernel,
        grid_spec=pltpu.PrefetchScalarGridSpec(
            num_scalar_prefetch=1,
            grid=(QUADS,),
            in_specs=[spec(k) for k in range(SLOTS * 4)],
            out_specs=pl.BlockSpec((1, SLOTS * T, 4 * T), lambda q, inv: (q, 0, 0)),
        ),
        out_shape=jax.ShapeDtypeStruct((QUADS, SLOTS * T, 4 * T), bf16),
        compiler_params=params(24),
        cost_estimate=pl.CostEstimate(flops=0, bytes_accessed=10 << 20, transcendentals=0),
        name="densify",
    )(inv, *([tile_values] * (SLOTS * 4)))


def tiles_kernel(band, a0, a1, a2, b0, b1, b2, inner, edge, low, high, acc):
    acc[...] = jnp.zeros_like(acc)
    for q in range(QUADS):
        rows = slice(q * T, (q + 1) * T)
        later = slice((QUADS + q) * T, (QUADS + q + 1) * T)
        sides = []
        for own, zed, pair in ((a0, a1, a2), (b0, b1, b2)):
            sides.append(jnp.concatenate([own[rows, :], pair[rows, :], zed[rows, :], pair[later, :]], axis=0))
        acc[q * T:(q + SLOTS) * T, :] += jnp.dot(
            band[q], jnp.concatenate(sides, axis=1), preferred_element_type=f32
        )
    low[...] = acc[0:2 * T, :].astype(bf16)
    high[...] = acc[10 * T:12 * T, :].astype(bf16)
    inner[...] = acc[4 * T:8 * T, :].astype(bf16)
    edge[0:2 * T, :] = acc[2 * T:4 * T, :]
    edge[2 * T:4 * T, :] = acc[8 * T:10 * T, :]


def tiles(band, first, second):
    return pl.pallas_call(
        tiles_kernel,
        in_specs=[VMEM] * 7,
        out_specs=[VMEM] * 4,
        out_shape=[
            jax.ShapeDtypeStruct((4 * T, 2 * T), bf16),
            jax.ShapeDtypeStruct((4 * T, 2 * T), f32),
            jax.ShapeDtypeStruct((2 * T, 2 * T), bf16),
            jax.ShapeDtypeStruct((2 * T, 2 * T), bf16),
        ],
        scratch_shapes=[pltpu.VMEM((12 * T, 2 * T), f32)],
        compiler_params=params(24),
        cost_estimate=pl.CostEstimate(flops=2 * 8 * 640 * 512 * 256, bytes_accessed=8 << 20, transcendentals=0),
        name="tiles",
    )(band, *first, *second)


def times_weight(depth, spread, weight, out, turned):
    for at, s in enumerate((0, 1, 3, 2)):
        src = pl.ds(pl.multiple_of(((depth[0] - s + 4) % 4) * T, T), T)
        turned[:, at * T:(at + 1) * T] = weight[:, src]
    got = lax.dot_general(spread, turned[...], (((1,), (1,)), ((), ())), preferred_element_type=f32).astype(bf16)
    for t in range(4):
        out[t] = got[:, t * T:(t + 1) * T]


def inner_kernel(depth, xa, xb, weight, out, turned):
    times_weight(depth, jnp.concatenate([xa[...], xb[...]], axis=1), weight, out, turned)


def edge_kernel(depth, xa, xb, na, nb, pa, pb, weight, out, turned):
    first, second = slice(0, T), slice(T, 2 * T)
    parts = (
        (xa, first, na, second, pb, first),
        (xa, second, nb, second, pa, first),
        (xb, first, na, first, pb, second),
        (xb, second, nb, first, pa, second),
    )
    chunks = []
    for x, at, n, n_at, p, p_at in parts:
        chunks.append(
            jnp.concatenate(
                [
                    (x[0:2 * T, at] + p[:, p_at].astype(f32)).astype(bf16),
                    (x[2 * T:4 * T, at] + n[:, n_at].astype(f32)).astype(bf16),
                ],
                axis=0,
            )
        )
    times_weight(depth, jnp.concatenate(chunks, axis=1), weight, out, turned)


def weighted(kernel, name, depth, arrays):
    return pl.pallas_call(
        kernel,
        in_specs=[SMEM] + [VMEM] * len(arrays),
        out_specs=VMEM,
        out_shape=jax.ShapeDtypeStruct((4, 4 * T, T), bf16),
        scratch_shapes=[pltpu.VMEM((4 * T, 4 * T), bf16)],
        compiler_params=params(16),
        cost_estimate=pl.CostEstimate(flops=2 * 512 * 512 * 512, bytes_accessed=3 << 20, transcendentals=0),
        name=name,
    )(depth, *arrays)


def outer_kernel(depth, agg, m0, m1, m2, m3, out, turned):
    for s, m in enumerate((m0, m1, m2, m3)):
        dst = pl.ds(pl.multiple_of(((depth[0] - s + 4) % 4) * T, T), T)
        turned[:, dst] = m[...]
    for a in range(4):
        got = lax.dot_general(
            agg[a], turned[...], (((0,), (0,)), ((), ())), preferred_element_type=f32
        ).astype(bf16)
        for t in range(4):
            out[a * 8:(a + 1) * 8, t] = got[:, t * T:(t + 1) * T].reshape(8, 16, T)


def outer(depth, agg, ms):
    return pl.pallas_call(
        outer_kernel,
        in_specs=[SMEM] + [VMEM] * 5,
        out_specs=VMEM,
        out_shape=jax.ShapeDtypeStruct((32, 4, 16, T), bf16),
        scratch_shapes=[pltpu.VMEM((8 * T, 4 * T), bf16)],
        compiler_params=params(16),
        cost_estimate=pl.CostEstimate(flops=2 * 512 * 512 * 1024, bytes_accessed=3 << 20, transcendentals=0),
        name="outer",
    )(depth, agg, *ms)


def inverse_table(rows, cols, count, stripe, col, depth):
    slot_ids = jnp.arange(rows.shape[0], dtype=jnp.int32)
    shift = (cols - (stripe * RB + rows) + BW) % NBLK
    within = rows % 32
    quad = within // 4
    slot = (within + shift - col) // 4 - quad
    key = (quad * SLOTS + slot) * 4 + ((rows % 4) ^ col)
    key = jnp.where((slot_ids < count) & (rows // 32 == depth), key, -1)
    targets = jnp.arange(QUADS * SLOTS * 4, dtype=jnp.int32)
    return jnp.max(jnp.where(key[None, :] == targets[:, None], slot_ids[None, :], -1), axis=1)


def local(out_grad, relu_mask, aggregated, weight, tile_values, tile_rows, tile_cols, tile_count):
    stripe = lax.axis_index("row")
    col = lax.axis_index("col")
    depth = lax.axis_index("depth")
    depth1 = depth.reshape(1).astype(jnp.int32)

    def quarter(array, t):
        return lax.dynamic_slice_in_dim(array, ((depth + t) % 4) * 1024, 1024, axis=0)

    def masked(t):
        return jnp.where(quarter(relu_mask, t) != 0, quarter(out_grad, t), jnp.zeros((), bf16))

    def from_depth(array, t):
        return lax.ppermute(array, "depth", ring(4, t))

    rows = [masked(0)] + [from_depth(masked(t), t) for t in (1, 2, 3)]
    whole_weight = lax.all_gather(weight, "depth", axis=1, tiled=True)

    inv = inverse_table(tile_rows[0, 0], tile_cols[0, 0], tile_count[0, 0], stripe, col, depth)
    band = densify(inv, tile_values)

    def spread_out(own):
        zed = lax.ppermute(own, "col", flip(2))
        pair = lax.ppermute(jnp.concatenate([own, zed], axis=0), "col", flip(1))
        return own, zed, pair

    chunks = {s: spread_out(rows[s]) for s in (0, 1, 3, 2)}
    inner_a, edge_a, low_a, high_a = tiles(band, chunks[0], chunks[1])
    next_a = lax.ppermute(low_a, RD, ring(32, -1))
    prev_a = lax.ppermute(high_a, RD, ring(32, 1))
    inner_b, edge_b, low_b, high_b = tiles(band, chunks[3], chunks[2])
    next_b = lax.ppermute(low_b, RD, ring(32, -1))
    prev_b = lax.ppermute(high_b, RD, ring(32, 1))

    inner = weighted(inner_kernel, "inner_rows", depth1, [inner_a, inner_b, whole_weight])
    inner = lax.all_to_all(inner, "depth", 0, 0)
    edge = weighted(
        edge_kernel, "edge_rows", depth1, [edge_a, edge_b, next_a, next_b, prev_a, prev_b, whole_weight]
    )
    edge = lax.all_to_all(edge, "depth", 0, 0)
    grad_input = jnp.concatenate([edge[:, :2 * T], inner, edge[:, 2 * T:]], axis=1).reshape(32 * T, T)

    late, _ = lax.optimization_barrier((aggregated, (rows[2], rows[3])))
    agg = lax.all_to_all(late.reshape(4, 8 * T, T), "depth", 0, 0)
    pieces = outer(depth1, agg, rows).reshape(128, 16, T)
    pieces = lax.all_to_all(pieces, ("row", "col", "depth"), 0, 0)
    piece = jnp.sum(pieces.astype(f32), axis=0)
    grad_weight = lax.all_to_all(jnp.broadcast_to(piece, (32, 16, T)), RC, 0, 0).reshape(4 * T, T)
    return grad_input, grad_weight


def solution(mesh):
    placed = (
        P(RC, "depth"),
        P(RC, "depth"),
        P(RC, "depth"),
        P(None, "depth"),
        P("row", "col", None, None, None),
        P("row", "col", None),
        P("row", "col", None),
        P("row", "col"),
    )
    return jax.shard_map(
        local,
        mesh=mesh,
        in_specs=placed,
        out_specs=(P(RC, "depth"), P(None, "depth")),
        check_vma=False,
    )
```

```python
import jax
import jax.numpy as jnp
from jax import lax
from jax.experimental import pallas as pl
from jax.experimental.pallas import tpu as pltpu
from jax.sharding import PartitionSpec as P

BW = 8
RB = 128
NBLK = 1024
T = 128
QUADS = 8
SLOTS = 5
RC = ("row", "col")
RD = ("row", "depth")
bf16 = jnp.bfloat16
SMALL = pl.CostEstimate(flops=1024, bytes_accessed=1024, transcendentals=0)
f32 = jnp.float32


def ring(n, shift):
    return [(i, (i + shift) % n) for i in range(n)]


def flip(bit):
    return [(i, i ^ bit) for i in range(4)]


def params(mib):
    return pltpu.CompilerParams(vmem_limit_bytes=mib << 20)


ANY = pl.BlockSpec(memory_space=pl.ANY)
SMEM = pl.BlockSpec(memory_space=pltpu.SMEM)
VMEM = pl.BlockSpec(memory_space=pltpu.VMEM)


def densify_kernel(inv, tiles, out, held, sem):
    per = SLOTS * 4

    for k in range(QUADS * per):
        at = inv[k]
        pltpu.make_async_copy(
            tiles.at[0, 0, jnp.where(at >= 0, at, k)], held.at[k // per, k % per], sem.at[k // per]
        ).start()
    for q in range(QUADS):
        pltpu.make_async_copy(held.at[q], held.at[q], sem.at[q]).wait()
        for k in range(per):
            slot, e = k // 4, k % 4
            turned = jnp.where(inv[q * per + k] >= 0, held[q, k].T, jnp.zeros((T, T), bf16))
            out[q, slot * T:(slot + 1) * T, e * T:(e + 1) * T] = turned


def densify(inv, tile_values):
    return pl.pallas_call(
        densify_kernel,
        in_specs=[SMEM, ANY],
        out_specs=VMEM,
        out_shape=jax.ShapeDtypeStruct((QUADS, SLOTS * T, 4 * T), bf16),
        scratch_shapes=[pltpu.VMEM((QUADS, SLOTS * 4, T, T), bf16), pltpu.SemaphoreType.DMA((QUADS,))],
        compiler_params=params(42),
        cost_estimate=SMALL,
        name="densify",
    )(inv, tile_values)


def columns_kernel(depth, band, n0, n1, n2, n3, f0, f1, f2, f3, w0, w1, w2, w3, *refs):
    parts, (acc, weight) = refs[0:4], refs[4:]
    for s, w in enumerate((w0, w1, w2, w3)):
        weight[:, s * T:(s + 1) * T] = w[8 * T:12 * T, :]
    acc[...] = jnp.zeros_like(acc)
    for q in range(QUADS):
        sides = [jnp.concatenate([part[q * T:(q + 1) * T] for part in (n0, n1, n2, n3)], axis=0)]
        for s in range(3):
            at = slice((8 * s + q) * T, (8 * s + q + 1) * T)
            sides.append(jnp.concatenate([part[at] for part in (f0, f1, f2, f3)], axis=0))
        acc[q * T:(q + SLOTS) * T, :] += jnp.dot(
            band[q], jnp.concatenate(sides, axis=1), preferred_element_type=f32
        )
    for k in range(6):
        rows = slice(k * 2 * T, (k + 1) * 2 * T)
        spread = acc[rows, :].astype(bf16)
        for t in range(4):
            src = pl.ds(pl.multiple_of((depth[0] + t) % 4 * T, T), T)
            got = lax.dot_general(
                spread, weight[src, :], (((1,), (1,)), ((), ())), preferred_element_type=f32
            ).astype(bf16)
            parts[t][rows, :] = got


def columns(depth, band, near, far, given):
    return pl.pallas_call(
        columns_kernel,
        in_specs=[SMEM] + [VMEM] * 13,
        out_specs=[VMEM] * 4,
        out_shape=[jax.ShapeDtypeStruct((12 * T, T), bf16)] * 4,
        scratch_shapes=[pltpu.VMEM((12 * T, 4 * T), f32), pltpu.VMEM((4 * T, 4 * T), bf16)],
        compiler_params=params(12),
        cost_estimate=SMALL,
        name="columns",
    )(depth, band, *near, *far, *given)


def place_kernel(depth, r0, r1, r2, r3, following, previous, out, ends):
    ends[0, 2 * T:4 * T] = previous[...]
    ends[5, 0:2 * T] = following[...]
    for t, part in enumerate((r0, r1, r2, r3)):
        k = (depth[0] - t + 4) % 4
        ends[k + 1, 0:2 * T] = part[0:2 * T, :]
        ends[k + 1, 2 * T:4 * T] = part[10 * T:12 * T, :]
    for t, part in enumerate((r0, r1, r2, r3)):
        k = (depth[0] - t + 4) % 4
        before = ends[k, 2 * T:4 * T].astype(f32)
        behind = ends[k + 2, 0:2 * T].astype(f32)
        out[k, 0:2 * T] = (part[2 * T:4 * T, :].astype(f32) + before).astype(bf16)
        out[k, 2 * T:6 * T] = part[4 * T:8 * T, :]
        out[k, 6 * T:8 * T] = (part[8 * T:10 * T, :].astype(f32) + behind).astype(bf16)


def place(depth, parts, following, previous):
    return pl.pallas_call(
        place_kernel,
        in_specs=[SMEM] + [VMEM] * 6,
        out_specs=VMEM,
        out_shape=jax.ShapeDtypeStruct((4, 8 * T, T), bf16),
        scratch_shapes=[pltpu.VMEM((6, 4 * T, T), bf16)],
        compiler_params=params(8),
        cost_estimate=SMALL,
        name="place",
    )(depth, *parts, following, previous)


def outer_kernel(depth, g0, g1, g2, g3, own, more, out, turned):
    for s in range(4):
        dst = pl.ds(pl.multiple_of(((depth[0] - s + 4) % 4) * T, T), T)
        turned[:, dst] = own[...] if s == 0 else more[(s - 1) * 8 * T:s * 8 * T, :]
    for s, g in enumerate((g0, g1, g2, g3)):
        a = (depth[0] - s + 4) % 4
        got = lax.dot_general(
            g[0:8 * T, :], turned[...], (((0,), (0,)), ((), ())), preferred_element_type=f32
        ).astype(bf16)
        for t in range(4):
            out[pl.ds(a * 8, 8), t] = got[:, t * T:(t + 1) * T].reshape(8, 16, T)


def outer(depth, given, own, more):
    return pl.pallas_call(
        outer_kernel,
        in_specs=[SMEM] + [VMEM] * 6,
        out_specs=VMEM,
        out_shape=jax.ShapeDtypeStruct((32, 4, 16, T), bf16),
        scratch_shapes=[pltpu.VMEM((8 * T, 4 * T), bf16)],
        compiler_params=params(8),
        cost_estimate=SMALL,
        name="outer",
    )(depth, *given, own, more)


def after(value, *others):
    return lax.optimization_barrier((value, others))[0]


def inverse_table(rows, cols, count, stripe, col, depth):
    slot_ids = jnp.arange(rows.shape[0], dtype=jnp.int32)
    shift = (cols - (stripe * RB + rows) + BW) % NBLK
    within = rows % 32
    quad = within // 4
    slot = (within + shift - col) // 4 - quad
    key = (quad * SLOTS + slot) * 4 + ((rows % 4) ^ col)
    key = jnp.where((slot_ids < count) & (rows // 32 == depth), key, -1)
    targets = jnp.arange(QUADS * SLOTS * 4, dtype=jnp.int32)
    return jnp.max(jnp.where(key[None, :] == targets[:, None], slot_ids[None, :], -1), axis=1)


def local(out_grad, relu_mask, aggregated, weight, tile_values, tile_rows, tile_cols, tile_count):
    stripe = lax.axis_index("row")
    col = lax.axis_index("col")
    depth = lax.axis_index("depth")

    def other(array):
        return lax.ppermute(array, "col", flip(2))

    def pair(array):
        return lax.ppermute(array, "col", flip(1))

    depth1 = depth.reshape(1).astype(jnp.int32)

    def quarter(array, t):
        return lax.dynamic_slice_in_dim(array, ((depth + t) % 4) * 1024, 1024)

    def masked(grads, mask, t):
        return jnp.where(quarter(mask, t) != 0, quarter(grads, t), jnp.zeros((), bf16))

    def from_depth(array, t):
        return lax.ppermute(array, "depth", ring(4, t))

    own = masked(out_grad, relu_mask, 0)
    zed = other(own)
    near = (own, pair(own), zed, pair(zed))
    grads, mask = after((out_grad, relu_mask), own)
    rows = {t: from_depth(masked(grads, mask, t), t) for t in (2, 1, 3)}

    more = jnp.concatenate([rows[1], rows[2], rows[3]], axis=0)
    zed = other(after(more, zed))
    late, late_weight = after((aggregated, weight), more)
    given = [jnp.concatenate([quarter(late, t), late_weight], axis=0) for t in range(4)]
    given = given[:1] + [from_depth(given[t], t) for t in (1, 2, 3)]
    inv = inverse_table(tile_rows[0, 0], tile_cols[0, 0], tile_count[0, 0], stripe, col, depth)
    band = densify(after(inv, more), tile_values)

    pieces = outer(depth1, given, own, more).reshape(128, 16, T)
    far = (more, pair(more), zed, pair(after(zed, band, pieces)))
    pieces = lax.all_to_all(pieces, ("row", "col", "depth"), 0, 0)

    res = columns(depth1, band, near, far, given)
    back = [res[0]] + [from_depth(res[t], t) for t in (1, 2, 3)]

    def of_quarter(k, rows):
        parts = [back[t][rows] for t in range(4)]
        t = (depth - k) % 4
        return jnp.where(t < 2, jnp.where(t == 0, parts[0], parts[1]), jnp.where(t == 2, parts[2], parts[3]))

    following = lax.ppermute(of_quarter(0, slice(0, 2 * T)), "row", ring(8, -1))
    previous = lax.ppermute(of_quarter(3, slice(10 * T, 12 * T)), "row", ring(8, 1))
    grad_input = place(depth1, back, following, previous).reshape(32 * T, T)

    piece = jnp.sum(after(pieces, res[0]).astype(f32), axis=0)
    grad_weight = lax.all_to_all(jnp.broadcast_to(piece, (32, 16, T)), RC, 0, 0).reshape(4 * T, T)
    return grad_input, grad_weight


def solution(mesh):
    placed = (
        P(RC, "depth"),
        P(RC, "depth"),
        P(RC, "depth"),
        P(None, "depth"),
        P("row", "col", None, None, None),
        P("row", "col", None),
        P("row", "col", None),
        P("row", "col"),
    )
    return jax.shard_map(
        local,
        mesh=mesh,
        in_specs=placed,
        out_specs=(P(RC, "depth"), P(None, "depth")),
        check_vma=False,
    )
```

```python
import jax
import jax.numpy as jnp
from jax import lax
from jax.experimental import pallas as pl
from jax.experimental.pallas import tpu as pltpu
from jax.sharding import PartitionSpec as P

BW = 8
RB = 128
NBLK = 1024
T = 128
QUADS = 8
SLOTS = 5
RC = ("row", "col")
RD = ("row", "depth")
bf16 = jnp.bfloat16
SMALL = pl.CostEstimate(flops=1024, bytes_accessed=1024, transcendentals=0)
f32 = jnp.float32


def ring(n, shift):
    return [(i, (i + shift) % n) for i in range(n)]


def flip(bit):
    return [(i, i ^ bit) for i in range(4)]


def params(mib):
    return pltpu.CompilerParams(vmem_limit_bytes=mib << 20)


ANY = pl.BlockSpec(memory_space=pl.ANY)
SMEM = pl.BlockSpec(memory_space=pltpu.SMEM)
VMEM = pl.BlockSpec(memory_space=pltpu.VMEM)


def densify_kernel(inv, tiles, out, held, sem):
    per = SLOTS * 4

    for k in range(QUADS * per):
        at = inv[k]
        pltpu.make_async_copy(
            tiles.at[0, 0, jnp.where(at >= 0, at, k)], held.at[k // per, k % per], sem.at[k // per]
        ).start()
    for q in range(QUADS):
        pltpu.make_async_copy(held.at[q], held.at[q], sem.at[q]).wait()
        for k in range(per):
            slot, e = k // 4, k % 4
            turned = jnp.where(inv[q * per + k] >= 0, held[q, k].T, jnp.zeros((T, T), bf16))
            out[q, slot * T:(slot + 1) * T, e * T:(e + 1) * T] = turned


def densify(inv, tile_values):
    return pl.pallas_call(
        densify_kernel,
        in_specs=[SMEM, ANY],
        out_specs=VMEM,
        out_shape=jax.ShapeDtypeStruct((QUADS, SLOTS * T, 4 * T), bf16),
        scratch_shapes=[pltpu.VMEM((QUADS, SLOTS * 4, T, T), bf16), pltpu.SemaphoreType.DMA((QUADS,))],
        compiler_params=params(42),
        cost_estimate=SMALL,
        name="densify",
    )(inv, tile_values)


def columns_kernel(depth, band, own, zed, pair, f0, f1, f2, f3, w0, w1, w2, w3, *refs):
    parts, (acc, weight) = refs[0:4], refs[4:]
    for t in range(4):
        src = pl.ds(pl.multiple_of(8 * T + (depth[0] + t) % 4 * T, T), T)
        for s, w in enumerate((w0, w1, w2, w3)):
            weight[t * T:(t + 1) * T, s * T:(s + 1) * T] = w[src, :]
    acc[...] = jnp.zeros_like(acc)
    for q in range(QUADS):
        here, later = slice(q * T, (q + 1) * T), slice((8 + q) * T, (9 + q) * T)
        sides = [jnp.concatenate([own[here], pair[here], zed[here], pair[later]], axis=0)]
        for s in range(3):
            at = slice((8 * s + q) * T, (8 * s + q + 1) * T)
            sides.append(jnp.concatenate([part[at] for part in (f0, f1, f2, f3)], axis=0))
        acc[q * T:(q + SLOTS) * T, :] += jnp.dot(
            band[q], jnp.concatenate(sides, axis=1), preferred_element_type=f32
        )
    for k in range(6):
        rows = slice(k * 2 * T, (k + 1) * 2 * T)
        got = lax.dot_general(
            acc[rows, :].astype(bf16), weight[...], (((1,), (1,)), ((), ())), preferred_element_type=f32
        ).astype(bf16)
        for t in range(4):
            parts[t][rows, :] = got[:, t * T:(t + 1) * T]


def columns(depth, band, near, far, given):
    return pl.pallas_call(
        columns_kernel,
        in_specs=[SMEM] + [VMEM] * 12,
        out_specs=[VMEM] * 4,
        out_shape=[jax.ShapeDtypeStruct((12 * T, T), bf16)] * 4,
        scratch_shapes=[pltpu.VMEM((12 * T, 4 * T), f32), pltpu.VMEM((4 * T, 4 * T), bf16)],
        compiler_params=params(12),
        cost_estimate=SMALL,
        name="columns",
    )(depth, band, *near, *far, *given)


def place_kernel(depth, r0, r1, r2, r3, following, previous, out, ends):
    ends[0, 2 * T:4 * T] = previous[...]
    ends[5, 0:2 * T] = following[...]
    for t, part in enumerate((r0, r1, r2, r3)):
        k = (depth[0] - t + 4) % 4
        ends[k + 1, 0:2 * T] = part[0:2 * T, :]
        ends[k + 1, 2 * T:4 * T] = part[10 * T:12 * T, :]
    for t, part in enumerate((r0, r1, r2, r3)):
        k = (depth[0] - t + 4) % 4
        before = ends[k, 2 * T:4 * T].astype(f32)
        behind = ends[k + 2, 0:2 * T].astype(f32)
        out[k, 0:2 * T] = (part[2 * T:4 * T, :].astype(f32) + before).astype(bf16)
        out[k, 2 * T:6 * T] = part[4 * T:8 * T, :]
        out[k, 6 * T:8 * T] = (part[8 * T:10 * T, :].astype(f32) + behind).astype(bf16)


def place(depth, parts, following, previous):
    return pl.pallas_call(
        place_kernel,
        in_specs=[SMEM] + [VMEM] * 6,
        out_specs=VMEM,
        out_shape=jax.ShapeDtypeStruct((4, 8 * T, T), bf16),
        scratch_shapes=[pltpu.VMEM((6, 4 * T, T), bf16)],
        compiler_params=params(8),
        cost_estimate=SMALL,
        name="place",
    )(depth, *parts, following, previous)


def outer_kernel(depth, g0, g1, g2, g3, own, more, out, turned):
    for s in range(4):
        dst = pl.ds(pl.multiple_of(((depth[0] - s + 4) % 4) * T, T), T)
        turned[:, dst] = own[...] if s == 0 else more[(s - 1) * 8 * T:s * 8 * T, :]
    for s, g in enumerate((g0, g1, g2, g3)):
        a = (depth[0] - s + 4) % 4
        got = lax.dot_general(
            g[0:8 * T, :], turned[...], (((0,), (0,)), ((), ())), preferred_element_type=f32
        ).astype(bf16)
        for t in range(4):
            out[pl.ds(a * 8, 8), t] = got[:, t * T:(t + 1) * T].reshape(8, 16, T)


def outer(depth, given, own, more):
    return pl.pallas_call(
        outer_kernel,
        in_specs=[SMEM] + [VMEM] * 6,
        out_specs=VMEM,
        out_shape=jax.ShapeDtypeStruct((32, 4, 16, T), bf16),
        scratch_shapes=[pltpu.VMEM((8 * T, 4 * T), bf16)],
        compiler_params=params(8),
        cost_estimate=SMALL,
        name="outer",
    )(depth, *given, own, more)


def after(value, *others):
    return lax.optimization_barrier((value, others))[0]


def inverse_table(rows, cols, count, stripe, col, depth):
    slot_ids = jnp.arange(rows.shape[0], dtype=jnp.int32)
    shift = (cols - (stripe * RB + rows) + BW) % NBLK
    within = rows % 32
    quad = within // 4
    slot = (within + shift - col) // 4 - quad
    key = (quad * SLOTS + slot) * 4 + ((rows % 4) ^ col)
    key = jnp.where((slot_ids < count) & (rows // 32 == depth), key, -1)
    targets = jnp.arange(QUADS * SLOTS * 4, dtype=jnp.int32)
    return jnp.max(jnp.where(key[None, :] == targets[:, None], slot_ids[None, :], -1), axis=1)


def local(out_grad, relu_mask, aggregated, weight, tile_values, tile_rows, tile_cols, tile_count):
    stripe = lax.axis_index("row")
    col = lax.axis_index("col")
    depth = lax.axis_index("depth")

    def other(array):
        return lax.ppermute(array, "col", flip(2))

    def pair(array):
        return lax.ppermute(array, "col", flip(1))

    depth1 = depth.reshape(1).astype(jnp.int32)

    def quarter(array, t):
        return lax.dynamic_slice_in_dim(array, ((depth + t) % 4) * 1024, 1024)

    def masked(grads, mask, t):
        return jnp.where(quarter(mask, t) != 0, quarter(grads, t), jnp.zeros((), bf16))

    def from_depth(array, t):
        return lax.ppermute(array, "depth", ring(4, t))

    own = masked(out_grad, relu_mask, 0)
    zed = other(own)
    near = (own, zed, pair(jnp.concatenate([own, zed], axis=0)))
    grads, mask = after((out_grad, relu_mask), own)
    rows = {t: from_depth(masked(grads, mask, t), t) for t in (2, 1, 3)}

    more = jnp.concatenate([rows[1], rows[2], rows[3]], axis=0)
    zed = other(after(more, zed))
    late, late_weight = after((aggregated, weight), rows[1])
    given = [jnp.concatenate([quarter(late, t), late_weight], axis=0) for t in range(4)]
    given = given[:1] + [from_depth(given[t], t) for t in (1, 2, 3)]
    inv = inverse_table(tile_rows[0, 0], tile_cols[0, 0], tile_count[0, 0], stripe, col, depth)
    band = densify(after(inv, more), tile_values)

    pieces = outer(after(depth1, band, near[2]), given, own, more).reshape(128, 16, T)
    far = (more, pair(more), zed, pair(after(zed, pieces)))
    pieces = lax.all_to_all(pieces, ("row", "col", "depth"), 0, 0)

    res = columns(depth1, band, near, far, given)
    back = [res[0]] + [from_depth(res[t], t) for t in (1, 2, 3)]

    def of_quarter(k, rows):
        parts = [back[t][rows] for t in range(4)]
        t = (depth - k) % 4
        return jnp.where(t < 2, jnp.where(t == 0, parts[0], parts[1]), jnp.where(t == 2, parts[2], parts[3]))

    following = lax.ppermute(of_quarter(0, slice(0, 2 * T)), "row", ring(8, -1))
    previous = lax.ppermute(of_quarter(3, slice(10 * T, 12 * T)), "row", ring(8, 1))
    grad_input = place(depth1, back, following, previous).reshape(32 * T, T)

    piece = jnp.sum(after(pieces, res[0]).astype(f32), axis=0)
    grad_weight = lax.all_to_all(jnp.broadcast_to(piece, (32, 16, T)), RC, 0, 0).reshape(4 * T, T)
    return grad_input, grad_weight


def solution(mesh):
    placed = (
        P(RC, "depth"),
        P(RC, "depth"),
        P(RC, "depth"),
        P(None, "depth"),
        P("row", "col", None, None, None),
        P("row", "col", None),
        P("row", "col", None),
        P("row", "col"),
    )
    return jax.shard_map(
        local,
        mesh=mesh,
        in_specs=placed,
        out_specs=(P(RC, "depth"), P(None, "depth")),
        check_vma=False,
    )
```

```python
import jax
import jax.numpy as jnp
from jax import lax
from jax.experimental import pallas as pl
from jax.experimental.pallas import tpu as pltpu
from jax.sharding import PartitionSpec as P

BW = 8
RB = 128
NBLK = 1024
T = 128
QUADS = 8
SLOTS = 5
RC = ("row", "col")
RD = ("row", "depth")
bf16 = jnp.bfloat16
SMALL = pl.CostEstimate(flops=1024, bytes_accessed=1024, transcendentals=0)
f32 = jnp.float32


def ring(n, shift):
    return [(i, (i + shift) % n) for i in range(n)]


def flip(bit):
    return [(i, i ^ bit) for i in range(4)]


def params(mib):
    return pltpu.CompilerParams(vmem_limit_bytes=mib << 20)


ANY = pl.BlockSpec(memory_space=pl.ANY)
SMEM = pl.BlockSpec(memory_space=pltpu.SMEM)
VMEM = pl.BlockSpec(memory_space=pltpu.VMEM)


def densify_kernel(inv, tiles, out, held, sem):
    per = SLOTS * 4

    for k in range(QUADS * per):
        at = inv[k]
        pltpu.make_async_copy(
            tiles.at[0, 0, jnp.where(at >= 0, at, k)], held.at[k // per, k % per], sem.at[k // per]
        ).start()
    for q in range(QUADS):
        pltpu.make_async_copy(held.at[q], held.at[q], sem.at[q]).wait()
        for k in range(per):
            slot, e = k // 4, k % 4
            turned = jnp.where(inv[q * per + k] >= 0, held[q, k].T, jnp.zeros((T, T), bf16))
            out[q, slot * T:(slot + 1) * T, e * T:(e + 1) * T] = turned


def densify(inv, tile_values):
    return pl.pallas_call(
        densify_kernel,
        in_specs=[SMEM, ANY],
        out_specs=VMEM,
        out_shape=jax.ShapeDtypeStruct((QUADS, SLOTS * T, 4 * T), bf16),
        scratch_shapes=[pltpu.VMEM((QUADS, SLOTS * 4, T, T), bf16), pltpu.SemaphoreType.DMA((QUADS,))],
        compiler_params=params(42),
        cost_estimate=SMALL,
        name="densify",
    )(inv, tile_values)


def columns_kernel(depth, band, own, zed, pair, f0, f1, f2, f3, w0, w1, w2, w3, *refs):
    parts, (acc, weight) = refs[0:4], refs[4:]
    for t in range(4):
        src = pl.ds(pl.multiple_of(8 * T + (depth[0] + t) % 4 * T, T), T)
        for s, w in enumerate((w0, w1, w2, w3)):
            weight[t * T:(t + 1) * T, s * T:(s + 1) * T] = w[src, :]
    for q in range(QUADS):
        here, later = slice(q * T, (q + 1) * T), slice((8 + q) * T, (9 + q) * T)
        sides = [jnp.concatenate([own[here], pair[here], zed[here], pair[later]], axis=0)]
        for s in range(3):
            at = slice((8 * s + q) * T, (8 * s + q + 1) * T)
            sides.append(jnp.concatenate([part[at] for part in (f0, f1, f2, f3)], axis=0))
        got = jnp.dot(band[q], jnp.concatenate(sides, axis=1), preferred_element_type=f32)
        seen = 0 if q == 0 else SLOTS - 1
        if seen:
            acc[q * T:(q + seen) * T, :] += got[0:seen * T]
        acc[(q + seen) * T:(q + SLOTS) * T, :] = got[seen * T:SLOTS * T]
    for k in range(6):
        rows = slice(k * 2 * T, (k + 1) * 2 * T)
        got = lax.dot_general(
            acc[rows, :].astype(bf16), weight[...], (((1,), (1,)), ((), ())), preferred_element_type=f32
        ).astype(bf16)
        for t in range(4):
            parts[t][rows, :] = got[:, t * T:(t + 1) * T]


def columns(depth, band, near, far, given):
    return pl.pallas_call(
        columns_kernel,
        in_specs=[SMEM] + [VMEM] * 12,
        out_specs=[VMEM] * 4,
        out_shape=[jax.ShapeDtypeStruct((12 * T, T), bf16)] * 4,
        scratch_shapes=[pltpu.VMEM((12 * T, 4 * T), f32), pltpu.VMEM((4 * T, 4 * T), bf16)],
        compiler_params=params(12),
        cost_estimate=SMALL,
        name="columns",
    )(depth, band, *near, *far, *given)


def place_kernel(depth, r0, r1, r2, r3, following, previous, grad_weight, out, out_weight, ends):
    out_weight[...] = grad_weight[...]
    ends[0, 2 * T:4 * T] = previous[...]
    ends[5, 0:2 * T] = following[...]
    for t, part in enumerate((r0, r1, r2, r3)):
        k = (depth[0] - t + 4) % 4
        ends[k + 1, 0:2 * T] = part[0:2 * T, :]
        ends[k + 1, 2 * T:4 * T] = part[10 * T:12 * T, :]
    for t, part in enumerate((r0, r1, r2, r3)):
        k = (depth[0] - t + 4) % 4
        before = ends[k, 2 * T:4 * T].astype(f32)
        behind = ends[k + 2, 0:2 * T].astype(f32)
        out[k, 0:2 * T] = (part[2 * T:4 * T, :].astype(f32) + before).astype(bf16)
        out[k, 2 * T:6 * T] = part[4 * T:8 * T, :]
        out[k, 6 * T:8 * T] = (part[8 * T:10 * T, :].astype(f32) + behind).astype(bf16)


def place(depth, parts, following, previous, grad_weight):
    return pl.pallas_call(
        place_kernel,
        in_specs=[SMEM] + [VMEM] * 7,
        out_specs=[VMEM] * 2,
        out_shape=[
            jax.ShapeDtypeStruct((4, 8 * T, T), bf16),
            jax.ShapeDtypeStruct((4 * T, T), f32),
        ],
        scratch_shapes=[pltpu.VMEM((6, 4 * T, T), bf16)],
        compiler_params=params(8),
        cost_estimate=SMALL,
        name="place",
    )(depth, *parts, following, previous, grad_weight)


def outer_kernel(depth, g0, g1, g2, g3, own, more, out, turned):
    for s in range(4):
        dst = pl.ds(pl.multiple_of(((depth[0] - s + 4) % 4) * T, T), T)
        turned[:, dst] = own[...] if s == 0 else more[(s - 1) * 8 * T:s * 8 * T, :]
    for s, g in enumerate((g0, g1, g2, g3)):
        a = (depth[0] - s + 4) % 4
        got = lax.dot_general(
            g[0:8 * T, :], turned[...], (((0,), (0,)), ((), ())), preferred_element_type=f32
        ).astype(bf16)
        for t in range(4):
            out[pl.ds(a * 8, 8), t] = got[:, t * T:(t + 1) * T].reshape(8, 16, T)


def outer(depth, given, own, more):
    return pl.pallas_call(
        outer_kernel,
        in_specs=[SMEM] + [VMEM] * 6,
        out_specs=VMEM,
        out_shape=jax.ShapeDtypeStruct((32, 4, 16, T), bf16),
        scratch_shapes=[pltpu.VMEM((8 * T, 4 * T), bf16)],
        compiler_params=params(8),
        cost_estimate=SMALL,
        name="outer",
    )(depth, *given, own, more)


def after(value, *others):
    return lax.optimization_barrier((value, others))[0]


def inverse_table(rows, cols, count, stripe, col, depth):
    slot_ids = jnp.arange(rows.shape[0], dtype=jnp.int32)
    shift = (cols - (stripe * RB + rows) + BW) % NBLK
    within = rows % 32
    quad = within // 4
    slot = (within + shift - col) // 4 - quad
    key = (quad * SLOTS + slot) * 4 + ((rows % 4) ^ col)
    key = jnp.where((slot_ids < count) & (rows // 32 == depth), key, -1)
    targets = jnp.arange(QUADS * SLOTS * 4, dtype=jnp.int32)
    return jnp.max(jnp.where(key[None, :] == targets[:, None], slot_ids[None, :], -1), axis=1)


def local(out_grad, relu_mask, aggregated, weight, tile_values, tile_rows, tile_cols, tile_count):
    stripe = lax.axis_index("row")
    col = lax.axis_index("col")
    depth = lax.axis_index("depth")

    def other(array):
        return lax.ppermute(array, "col", flip(2))

    def pair(array):
        return lax.ppermute(array, "col", flip(1))

    depth1 = depth.reshape(1).astype(jnp.int32)

    def quarter(array, t):
        return lax.dynamic_slice_in_dim(array, ((depth + t) % 4) * 1024, 1024)

    def masked(grads, mask, t):
        return jnp.where(quarter(mask, t) != 0, quarter(grads, t), jnp.zeros((), bf16))

    def from_depth(array, t):
        return lax.ppermute(array, "depth", ring(4, t))

    own = masked(out_grad, relu_mask, 0)
    zed = other(own)
    near = (own, zed, pair(jnp.concatenate([own, zed], axis=0)))
    grads, mask = after((out_grad, relu_mask), own)
    rows = {t: from_depth(masked(grads, mask, t), t) for t in (2, 1, 3)}

    more = jnp.concatenate([rows[1], rows[2], rows[3]], axis=0)
    zed = other(after(more, zed))
    late, late_weight = after((aggregated, weight), rows[1])
    given = [jnp.concatenate([quarter(late, t), late_weight], axis=0) for t in range(4)]
    given = given[:1] + [from_depth(given[t], t) for t in (1, 2, 3)]
    inv = inverse_table(tile_rows[0, 0], tile_cols[0, 0], tile_count[0, 0], stripe, col, depth)
    band = densify(after(inv, more), tile_values)

    pieces = outer(after(depth1, band, near[2]), given, own, more).reshape(128, 16, T)
    far = (more, pair(more), zed, pair(after(zed, pieces)))
    pieces = lax.all_to_all(pieces, ("row", "col", "depth"), 0, 0)

    res = columns(depth1, band, near, far, given)
    back = [res[0]] + [from_depth(res[t], t) for t in (1, 2, 3)]

    def of_quarter(k, rows):
        parts = [back[t][rows] for t in range(4)]
        t = (depth - k) % 4
        return jnp.where(t < 2, jnp.where(t == 0, parts[0], parts[1]), jnp.where(t == 2, parts[2], parts[3]))

    following = lax.ppermute(of_quarter(0, slice(0, 2 * T)), "row", ring(8, -1))
    previous = lax.ppermute(of_quarter(3, slice(10 * T, 12 * T)), "row", ring(8, 1))

    piece = jnp.sum(after(pieces, res[0]).astype(f32), axis=0)
    grad_weight = lax.all_to_all(jnp.broadcast_to(piece, (32, 16, T)), RC, 0, 0).reshape(4 * T, T)
    grad_input, grad_weight = place(depth1, back, following, previous, grad_weight)
    return grad_input.reshape(32 * T, T), grad_weight


def solution(mesh):
    placed = (
        P(RC, "depth"),
        P(RC, "depth"),
        P(RC, "depth"),
        P(None, "depth"),
        P("row", "col", None, None, None),
        P("row", "col", None),
        P("row", "col", None),
        P("row", "col"),
    )
    return jax.shard_map(
        local,
        mesh=mesh,
        in_specs=placed,
        out_specs=(P(RC, "depth"), P(None, "depth")),
        check_vma=False,
    )
```

```python
import jax
import jax.numpy as jnp
from jax import lax
from jax.experimental import pallas as pl
from jax.experimental.pallas import tpu as pltpu
from jax.sharding import PartitionSpec as P

BW = 8
RB = 128
NBLK = 1024
T = 128
QUADS = 8
SLOTS = 5
RC = ("row", "col")
RD = ("row", "depth")
bf16 = jnp.bfloat16
SMALL = pl.CostEstimate(flops=1024, bytes_accessed=1024, transcendentals=0)
f32 = jnp.float32


def ring(n, shift):
    return [(i, (i + shift) % n) for i in range(n)]


def flip(bit):
    return [(i, i ^ bit) for i in range(4)]


def params(mib):
    return pltpu.CompilerParams(vmem_limit_bytes=mib << 20)


ANY = pl.BlockSpec(memory_space=pl.ANY)
SMEM = pl.BlockSpec(memory_space=pltpu.SMEM)
VMEM = pl.BlockSpec(memory_space=pltpu.VMEM)


def densify_kernel(inv, tiles, out, held, sem):
    per = SLOTS * 4

    for k in range(QUADS * per):
        at = inv[k]
        pltpu.make_async_copy(
            tiles.at[0, 0, jnp.where(at >= 0, at, k)], held.at[k // per, k % per], sem.at[k // per]
        ).start()
    for q in range(QUADS):
        pltpu.make_async_copy(held.at[q], held.at[q], sem.at[q]).wait()
        for k in range(per):
            slot, e = k // 4, k % 4
            turned = jnp.where(inv[q * per + k] >= 0, held[q, k].T, jnp.zeros((T, T), bf16))
            out[q, slot * T:(slot + 1) * T, e * T:(e + 1) * T] = turned


def densify(inv, tile_values):
    return pl.pallas_call(
        densify_kernel,
        in_specs=[SMEM, ANY],
        out_specs=VMEM,
        out_shape=jax.ShapeDtypeStruct((QUADS, SLOTS * T, 4 * T), bf16),
        scratch_shapes=[pltpu.VMEM((QUADS, SLOTS * 4, T, T), bf16), pltpu.SemaphoreType.DMA((QUADS,))],
        compiler_params=params(42),
        cost_estimate=SMALL,
        name="densify",
    )(inv, tile_values)


def columns_kernel(depth, band, own, zed, pair, f0, f1, f2, f3, w0, w1, w2, w3, *refs):
    parts, (acc, weight) = refs[0:4], refs[4:]
    for t in range(4):
        src = pl.ds(pl.multiple_of(8 * T + (depth[0] + t) % 4 * T, T), T)
        for s, w in enumerate((w0, w1, w2, w3)):
            weight[t * T:(t + 1) * T, s * T:(s + 1) * T] = w[src, :]

    def finish(k):
        rows = slice(k * 2 * T, (k + 1) * 2 * T)
        got = lax.dot_general(
            acc[rows, :].astype(bf16), weight[...], (((1,), (1,)), ((), ())), preferred_element_type=f32
        ).astype(bf16)
        for t in range(4):
            parts[t][rows, :] = got[:, t * T:(t + 1) * T]

    for q in range(QUADS):
        here, later = slice(q * T, (q + 1) * T), slice((8 + q) * T, (9 + q) * T)
        sides = [jnp.concatenate([own[here], pair[here], zed[here], pair[later]], axis=0)]
        for s in range(3):
            at = slice((8 * s + q) * T, (8 * s + q + 1) * T)
            sides.append(jnp.concatenate([part[at] for part in (f0, f1, f2, f3)], axis=0))
        got = jnp.dot(band[q], jnp.concatenate(sides, axis=1), preferred_element_type=f32)
        seen = 0 if q == 0 else SLOTS - 1
        if seen:
            acc[q * T:(q + seen) * T, :] += got[0:seen * T]
        acc[(q + seen) * T:(q + SLOTS) * T, :] = got[seen * T:SLOTS * T]
        if q % 2:
            finish(q // 2)
    finish(4)
    finish(5)


def columns(depth, band, near, far, given):
    return pl.pallas_call(
        columns_kernel,
        in_specs=[SMEM] + [VMEM] * 12,
        out_specs=[VMEM] * 4,
        out_shape=[jax.ShapeDtypeStruct((12 * T, T), bf16)] * 4,
        scratch_shapes=[pltpu.VMEM((12 * T, 4 * T), f32), pltpu.VMEM((4 * T, 4 * T), bf16)],
        compiler_params=params(12),
        cost_estimate=SMALL,
        name="columns",
    )(depth, band, *near, *far, *given)


def place_kernel(depth, r0, r1, r2, r3, following, previous, grad_weight, out, out_weight, ends):
    out_weight[...] = grad_weight[...]
    ends[0, 2 * T:4 * T] = previous[...]
    ends[5, 0:2 * T] = following[...]
    for t, part in enumerate((r0, r1, r2, r3)):
        k = (depth[0] - t + 4) % 4
        ends[k + 1, 0:2 * T] = part[0:2 * T, :]
        ends[k + 1, 2 * T:4 * T] = part[10 * T:12 * T, :]
    for t, part in enumerate((r0, r1, r2, r3)):
        k = (depth[0] - t + 4) % 4
        before = ends[k, 2 * T:4 * T].astype(f32)
        behind = ends[k + 2, 0:2 * T].astype(f32)
        out[k, 0:2 * T] = (part[2 * T:4 * T, :].astype(f32) + before).astype(bf16)
        out[k, 2 * T:6 * T] = part[4 * T:8 * T, :]
        out[k, 6 * T:8 * T] = (part[8 * T:10 * T, :].astype(f32) + behind).astype(bf16)


def place(depth, parts, following, previous, grad_weight):
    return pl.pallas_call(
        place_kernel,
        in_specs=[SMEM] + [VMEM] * 7,
        out_specs=[VMEM] * 2,
        out_shape=[
            jax.ShapeDtypeStruct((4, 8 * T, T), bf16),
            jax.ShapeDtypeStruct((4 * T, T), f32),
        ],
        scratch_shapes=[pltpu.VMEM((6, 4 * T, T), bf16)],
        compiler_params=params(8),
        cost_estimate=SMALL,
        name="place",
    )(depth, *parts, following, previous, grad_weight)


def outer_kernel(depth, g0, g1, g2, g3, own, more, out, turned):
    for s in range(4):
        dst = pl.ds(pl.multiple_of(((depth[0] - s + 4) % 4) * T, T), T)
        turned[:, dst] = own[...] if s == 0 else more[(s - 1) * 8 * T:s * 8 * T, :]
    for s, g in enumerate((g0, g1, g2, g3)):
        a = (depth[0] - s + 4) % 4
        got = lax.dot_general(
            g[0:8 * T, :], turned[...], (((0,), (0,)), ((), ())), preferred_element_type=f32
        ).astype(bf16)
        for t in range(4):
            out[pl.ds(a * 8, 8), t] = got[:, t * T:(t + 1) * T].reshape(8, 16, T)


def outer(depth, given, own, more):
    return pl.pallas_call(
        outer_kernel,
        in_specs=[SMEM] + [VMEM] * 6,
        out_specs=VMEM,
        out_shape=jax.ShapeDtypeStruct((32, 4, 16, T), bf16),
        scratch_shapes=[pltpu.VMEM((8 * T, 4 * T), bf16)],
        compiler_params=params(8),
        cost_estimate=SMALL,
        name="outer",
    )(depth, *given, own, more)


def after(value, *others):
    return lax.optimization_barrier((value, others))[0]


def inverse_table(rows, cols, count, stripe, col, depth):
    slot_ids = jnp.arange(rows.shape[0], dtype=jnp.int32)
    shift = (cols - (stripe * RB + rows) + BW) % NBLK
    within = rows % 32
    quad = within // 4
    slot = (within + shift - col) // 4 - quad
    key = (quad * SLOTS + slot) * 4 + ((rows % 4) ^ col)
    key = jnp.where((slot_ids < count) & (rows // 32 == depth), key, -1)
    targets = jnp.arange(QUADS * SLOTS * 4, dtype=jnp.int32)
    return jnp.max(jnp.where(key[None, :] == targets[:, None], slot_ids[None, :], -1), axis=1)


def local(out_grad, relu_mask, aggregated, weight, tile_values, tile_rows, tile_cols, tile_count):
    stripe = lax.axis_index("row")
    col = lax.axis_index("col")
    depth = lax.axis_index("depth")

    def other(array):
        return lax.ppermute(array, "col", flip(2))

    def pair(array):
        return lax.ppermute(array, "col", flip(1))

    depth1 = depth.reshape(1).astype(jnp.int32)

    def quarter(array, t):
        return lax.dynamic_slice_in_dim(array, ((depth + t) % 4) * 1024, 1024)

    def masked(grads, mask, t):
        return jnp.where(quarter(mask, t) != 0, quarter(grads, t), jnp.zeros((), bf16))

    def from_depth(array, t):
        return lax.ppermute(array, "depth", ring(4, t))

    own = masked(out_grad, relu_mask, 0)
    zed = other(own)
    near = (own, zed, pair(jnp.concatenate([own, zed], axis=0)))
    grads, mask = after((out_grad, relu_mask), own)
    rows = {t: from_depth(masked(grads, mask, t), t) for t in (2, 1, 3)}

    more = jnp.concatenate([rows[1], rows[2], rows[3]], axis=0)
    zed = other(after(more, zed))
    late, late_weight = after((aggregated, weight), rows[1])
    given = [jnp.concatenate([quarter(late, t), late_weight], axis=0) for t in range(4)]
    given = given[:1] + [from_depth(given[t], t) for t in (1, 2, 3)]
    inv = inverse_table(tile_rows[0, 0], tile_cols[0, 0], tile_count[0, 0], stripe, col, depth)
    band = densify(after(inv, more), tile_values)

    pieces = outer(after(depth1, band, near[2]), given, own, more).reshape(128, 16, T)
    far = (more, pair(more), zed, pair(after(zed, pieces)))
    pieces = lax.all_to_all(pieces, ("row", "col", "depth"), 0, 0)

    res = columns(depth1, band, near, far, given)
    back = [res[0]] + [from_depth(res[t], t) for t in (1, 2, 3)]

    def of_quarter(k, rows):
        parts = [back[t][rows] for t in range(4)]
        t = (depth - k) % 4
        return jnp.where(t < 2, jnp.where(t == 0, parts[0], parts[1]), jnp.where(t == 2, parts[2], parts[3]))

    following = lax.ppermute(of_quarter(0, slice(0, 2 * T)), "row", ring(8, -1))
    previous = lax.ppermute(of_quarter(3, slice(10 * T, 12 * T)), "row", ring(8, 1))

    piece = jnp.sum(after(pieces, res[0]).astype(f32), axis=0)
    grad_weight = lax.all_to_all(jnp.broadcast_to(piece, (32, 16, T)), RC, 0, 0).reshape(4 * T, T)
    grad_input, grad_weight = place(depth1, back, following, previous, grad_weight)
    return grad_input.reshape(32 * T, T), grad_weight


def solution(mesh):
    placed = (
        P(RC, "depth"),
        P(RC, "depth"),
        P(RC, "depth"),
        P(None, "depth"),
        P("row", "col", None, None, None),
        P("row", "col", None),
        P("row", "col", None),
        P("row", "col"),
    )
    return jax.shard_map(
        local,
        mesh=mesh,
        in_specs=placed,
        out_specs=(P(RC, "depth"), P(None, "depth")),
        check_vma=False,
    )
```
